32 devices in a mesh: dp: 4 (over z), segment: 2 (over x), chan: 4 (over y, core).
Axes of the slice: x: 2, y: 2, z: 4, core: 2. Of those that a mesh axis runs over, the one named last changes fastest.
Arguments:
- base: bfloat16 [8, 512, 256], P('dp', 'chan'), may hold values from -6 to 6
- style: float32 [2, 8, 512], P('segment', 'dp'), may hold values from -3 to 3
- noise: float32 [2, 8, 256], P('segment', 'dp'), may hold values from -6 to 6
- conv_weight: bfloat16 [2, 4608, 512], P('segment', None, 'chan'), may hold values from -0.09375 to 0.09375
- conv_bias: float32 [2, 512], P('segment', 'chan'), may hold values from -3 to 3
- noise_gain: float32 [2, 512], P('segment', 'chan'), may hold values from 0.1 to 1
- rgb_weight: bfloat16 [2, 3, 512], P('segment', None, 'chan'), may hold values from -0.25 to 0.25
- disc_weight: float32 [3, 256], replicated, may hold values from -3.5 to 3.5
- disc_bias: float32 [256], replicated, may hold values from -3 to 3
- disc_out: float32 [256], replicated, may hold values from -3 to 3
Outputs:
- conv_grad: float32 [2, 4608, 512], P('segment', 'dp', 'chan')
- logits: float32 [8], P('dp')
- section_input_grads: bfloat16 [2, 8, 512, 256], P('segment', 'dp', 'chan')
The draws below stay inside these ranges and needn't reach their ends.
All inputs are finite; a program needn't handle non-finite values.
Results may differ from the reference program's by a relative error of at most 0.015.
Values may be sent and summed in bfloat16 or wider, within the bound.
A program may use at most 64 MiB of HBM per device.

```python
import math
import jax
import jax.numpy as jnp
from jax import lax

C = 512
CD = 256
RES = 16
PIX = 256
BATCH = 8


def draw_style(key, part):
    sign_key, size_key = jax.random.split(jax.random.fold_in(key, 11))
    sign_values = (2 * jax.random.randint(sign_key, (2, BATCH, C), 0, 2) - 1).astype(jnp.float32)
    exponent = jax.random.uniform(size_key, (2, BATCH, C), jnp.float32, math.log(0.3), math.log(3.0))
    magnitude = jnp.clip(jnp.exp(exponent), 0.3, 3.0)
    return sign_values * magnitude


def draw_conv_bias(key, part):
    first_key, second_key = jax.random.split(jax.random.fold_in(key, 23))
    first_row = jax.random.uniform(first_key, (C,), jnp.float32, -1.55, -1.25)
    second_row = jnp.clip(0.5 * jax.random.normal(second_key, (C,), jnp.float32), -3.0, 3.0)
    return jnp.stack([first_row, second_row])


def block_scale(key, dims, pieces, least, top_value):
    factor_of = 1.0
    for dim, parts in pieces:
        draws = jax.random.uniform(jax.random.fold_in(jax.random.fold_in(key, 6), dim), (parts,), jnp.float32, least / len(pieces), top_value / len(pieces))
        factor_of = factor_of * jnp.repeat(jnp.exp(draws), dims[dim] // parts).reshape((-1,) + (1,) * (len(dims) - 1 - dim))
    return factor_of


def scatter_about(stream_key, extent, scale, reach, cuts=(), kind=jnp.bfloat16):
    result = jax.random.normal(stream_key, extent, jnp.float32) * scale
    if len(cuts) > 0:
        result = block_scale(stream_key, extent, cuts, -0.22, 0.18) * result
    return jnp.clip(result, min=-reach, max=reach).astype(kind)


def setup_inputs(seed: int = 0) -> dict:
    streams_of = jax.random.split(jax.random.key(seed), 11)
    return {
        "base": scatter_about(streams_of[0], (BATCH, C, PIX), 1.0, 6.0, ((0, 4), (1, 4))),
        "style": draw_style(jax.random.fold_in(streams_of[10], 71), 0),
        "noise": scatter_about(streams_of[2], (2, BATCH, PIX), 1.0, 6.0, ((0, 2), (1, 4)), jnp.float32),
        "conv_weight": scatter_about(streams_of[3], (2, 9 * C, C), (9 * C) ** -0.5, 0.09375, ((0, 2), (2, 4))),
        "conv_bias": draw_conv_bias(jax.random.fold_in(streams_of[10], 71), 0),
        "noise_gain": jnp.clip(jnp.exp(math.log(1.0) - 2.3025851 * jax.random.uniform(streams_of[5], (2, C), jnp.float32) ** block_scale(streams_of[5], (2, C), ((0, 2), (1, 4)), -0.2, 0.2)), 0.1, 1.0),
        "rgb_weight": scatter_about(streams_of[6], (2, 3, C), C ** -0.5, 0.25, ((0, 2), (2, 4))),
        "disc_weight": scatter_about(streams_of[7], (3, CD), 3 ** -0.5, 3.5, (), jnp.float32),
        "disc_bias": scatter_about(streams_of[8], (CD,), 0.5, 3.0, (), jnp.float32),
        "disc_out": scatter_about(streams_of[9], (CD,), 0.5, 3.0, (), jnp.float32),
    }


epsilon = 1e-06
root_two = 1.4142135623730951
highest = lax.Precision.HIGHEST
kernel_offsets = [(ky - 1, kx - 1) for ky in range(3) for kx in range(3)]

def leaky_relu(values):
    return 0.2 * values + 0.8 * jax.nn.softplus(values)

def leaky_slope(values):
    return 0.2 + 0.8 * jax.nn.sigmoid(values)

def shift_grid(values, offset_y, offset_x):
    leading = values.shape[:-1]
    planes = values.reshape(leading + (RES, RES))
    padded = jnp.pad(planes, [(0, 0)] * len(leading) + [(1, 1), (1, 1)])
    moved = padded[..., 1 + offset_y:1 + offset_y + RES, 1 + offset_x:1 + offset_x + RES]
    return moved.reshape(leading + (RES * RES,))

def unfold(modulated):
    return jnp.concatenate([shift_grid(modulated, oy, ox) for oy, ox in kernel_offsets], axis=0)

def fold_back(columns, channels):
    total = jnp.zeros((channels, RES * RES), columns.dtype)
    for kernel_pos, (oy, ox) in enumerate(kernel_offsets):
        total = total + shift_grid(columns[kernel_pos * channels:(kernel_pos + 1) * channels], -oy, -ox)
    return total

def section_forward(inputs, style_row, noise_row, weight, bias_row, gain_row):
    w_float = weight.astype(jnp.float32)
    squares = lax.optimization_barrier(jnp.sum((w_float * w_float).reshape(9, C, C), axis=0))
    demod = lax.rsqrt(jnp.dot(style_row * style_row, squares, precision=highest, preferred_element_type=jnp.float32) + epsilon)
    modulated = (inputs.astype(jnp.float32) * style_row[:, None]).astype(jnp.bfloat16)
    columns = unfold(modulated)
    conv_out = lax.dot_general(weight, columns, (((0,), (0,)), ((), ())), preferred_element_type=jnp.float32)
    pre_act = demod[:, None] * conv_out + gain_row[:, None] * noise_row[None, :] + bias_row[:, None]
    out_act = (root_two * leaky_relu(pre_act)).astype(jnp.bfloat16)
    return (out_act, pre_act, conv_out, demod, columns)

def section_backward(grad_out, pre_act, conv_out, demod, weight, style_row, columns):
    d_act = grad_out * root_two * leaky_slope(pre_act)
    d_conv = (d_act * demod[:, None]).astype(jnp.bfloat16)
    d_demod = lax.optimization_barrier(jnp.sum(d_act * conv_out, axis=1))
    coef = -d_demod * demod * demod * demod
    d_columns = lax.dot_general(weight, d_conv, (((1,), (0,)), ((), ())), preferred_element_type=jnp.float32)
    d_input = fold_back(d_columns, C)
    returned = (d_input * style_row[:, None]).astype(jnp.bfloat16)
    w_float = weight.astype(jnp.float32)
    outer = (style_row * style_row)[:, None] * coef[None, :]
    grad = lax.dot_general(columns, d_conv, (((1,), (1,)), ((), ())), preferred_element_type=jnp.float32)
    grad = grad + (w_float.reshape(9, C, C) * outer[None]).reshape(9 * C, C)
    return (returned, grad)

def reference(base, style, noise, conv_weight, conv_bias, noise_gain, rgb_weight, disc_weight, disc_bias, disc_out):
    styles = jnp.swapaxes(style, 0, 1)
    noises = jnp.swapaxes(noise, 0, 1)

    def one_sample(carry, items):
        sample_base, sample_style, sample_noise = items
        first = section_forward(sample_base, sample_style[0], sample_noise[0], conv_weight[0], conv_bias[0], noise_gain[0])
        second = section_forward(first[0], sample_style[1], sample_noise[1], conv_weight[1], conv_bias[1], noise_gain[1])
        image = jnp.dot(rgb_weight[0], first[0], preferred_element_type=jnp.float32)
        image = image + jnp.dot(rgb_weight[1], second[0], preferred_element_type=jnp.float32)
        pre_disc = jnp.einsum('cj,cp->jp', disc_weight, image, precision=highest) + disc_bias[:, None]
        hidden = leaky_relu(pre_disc)
        logit = jnp.dot(disc_out, lax.optimization_barrier(jnp.mean(hidden, axis=1)), precision=highest)
        grad_logit = jax.nn.sigmoid(logit) - 1.0
        d_pre = grad_logit * disc_out[:, None] / (RES * RES) * leaky_slope(pre_disc)
        d_image = jnp.einsum('cj,jp->cp', disc_weight, d_pre, precision=highest)
        head_second = jnp.einsum('co,cp->op', rgb_weight[1].astype(jnp.float32), d_image, precision=highest)
        head_first = jnp.einsum('co,cp->op', rgb_weight[0].astype(jnp.float32), d_image, precision=highest)
        returned, grad_second = section_backward(head_second, second[1], second[2], second[3], conv_weight[1], sample_style[1], second[4])
        grad_in = head_first + returned.astype(jnp.float32)
        first_returned, grad_first = section_backward(grad_in, first[1], first[2], first[3], conv_weight[0], sample_style[0], first[4])
        return ((carry[0] + grad_first, carry[1] + grad_second), (logit, jnp.stack([first_returned, returned])))
    zeros = jnp.zeros((9 * C, C), jnp.float32)
    totals, outputs = lax.scan(one_sample, (zeros, zeros), (base, styles, noises))
    logits, input_grads = outputs
    return (jnp.stack([totals[0], totals[1]]), logits, jnp.swapaxes(input_grads, 0, 1))
```

```python
import functools
import math
import jax
import jax.numpy as jnp
from jax import lax
from jax.experimental import pallas as pl
from jax.experimental.pallas import tpu as pltpu
from jax.sharding import PartitionSpec as P

epsilon = 1e-06
root_two = 1.4142135623730951
f32 = jnp.float32
bf16 = jnp.bfloat16
MESH = pl.DeviceIdType.MESH
OFFSETS = [(ky - 1, kx - 1) for ky in range(3) for kx in range(3)]


def leaky_pair(t):
    e = jnp.exp(-jnp.abs(t))
    act = 0.2 * t + 0.8 * (jnp.maximum(t, 0.0) + jnp.log1p(e))
    slope = 0.2 + 0.8 * (jnp.where(t >= 0.0, 1.0, e) / (1.0 + e))
    return act, slope


def remote(src, dst, send_sem, recv_sem, dev):
    return pltpu.make_async_remote_copy(
        src_ref=src,
        dst_ref=dst,
        send_sem=send_sem,
        recv_sem=recv_sem,
        device_id=dev,
        device_id_type=MESH,
    )


def kernel(
    nd,
    nc,
    base_ref,
    style_ref,
    noise_ref,
    w_ref,
    bias_ref,
    gain_ref,
    rgb_ref,
    dw_ref,
    db_ref,
    do_ref,
    grad_out,
    logit_out,
    ret_out,
    pack,
    cols,
    dpack,
    dcols,
    wt,
    wcat,
    demods,
    yin,
    ytx,
    xfull,
    styall,
    coefall,
    conv_s,
    pre_s,
    img,
    dimg,
    gzall,
    gst,
    tx,
    rx,
    dxown,
    retbuf,
    rettx,
    gt,
    dmat,
    xg_s,
    xg_r,
    xd_s,
    xd_r,
    xf_s,
    xf_r,
    im_s,
    im_r,
    yy_s,
    yy_r,
    rs_s,
    rs_r,
    rt_s,
    rt_r,
    gz_s,
    gz_r,
    cf_s,
    cf_r,
    st_s,
    st_r,
):
    dp = lax.axis_index("dp")
    seg = lax.axis_index("segment")
    ch = lax.axis_index("chan")
    mb, ow, px = base_ref.shape
    full = w_ref.shape[1] // 9
    res = math.isqrt(px)
    nb = nd * mb
    ng = 2 * nc

    def at(d, s, c):
        return {"dp": d, "segment": s, "chan": c}

    def chan_peer(j):
        return lax.rem(ch + j, nc)

    def chan_from(j):
        return lax.rem(ch + nc - j, nc)

    def dp_peer(j):
        return lax.rem(dp + j, nd)

    def dp_from(j):
        return lax.rem(dp + nd - j, nd)

    me_group = seg * nc + ch

    barrier = pltpu.get_barrier_semaphore()
    for j in range(1, ng):
        g = lax.rem(me_group + j, ng)
        pl.semaphore_signal(
            barrier, inc=1, device_id=at(dp, g // nc, lax.rem(g, nc)), device_id_type=MESH
        )
    for j in range(1, nd):
        pl.semaphore_signal(barrier, inc=1, device_id=at(dp_peer(j), seg, ch), device_id_type=MESH)

    pack[...] = jnp.zeros_like(pack)
    pack[0:3, :] = rgb_ref[0].astype(f32)
    pack[3:4, :] = bias_ref[...]
    pack[4:5, :] = gain_ref[...]
    pack[5 : 5 + mb, :] = style_ref[0, :, pl.ds(pl.multiple_of(ch * ow, ow), ow)]
    cols[...] = pack[...].T

    def own_x(d, m):
        return xfull.at[
            pl.ds(pl.multiple_of(ch * ow, ow), ow),
            pl.ds(pl.multiple_of((d * mb + m) * px, px), px),
        ]

    def x_block(d, m, c, n=1):
        return xfull.at[
            pl.ds(pl.multiple_of(c * ow, ow), ow),
            pl.ds(pl.multiple_of((d * mb + m) * px, px), n * px),
        ]

    pairs = nc // 2
    pair, core = ch // 2, lax.rem(ch, 2)
    other = pair * 2 + 1 - core

    def same_core(q):
        return lax.rem(pair + q, pairs) * 2 + core

    def came_from(q, c):
        return lax.rem(pair + pairs - q, pairs) * 2 + c

    def gather_out(block, sends, recvs):
        ops = [remote(block(ch), block(ch), sends(q), recvs(q), at(dp, seg, same_core(q)))
               for q in range(1, pairs)]
        return ops + [remote(block(ch), block(ch), sends(0), recvs(0), at(dp, seg, other))]

    def gather_relay(block, sends, recvs):
        ops = []
        for q in range(1, pairs):
            i = pairs - 1 + q
            ref = block(came_from(q, core))
            ops.append(remote(ref, ref, sends(i), recvs(i), at(dp, seg, other)))
        return ops

    def relay_in(block, sends, recvs):
        ops = []
        for q in range(1, pairs):
            ref = block(came_from(q, core))
            ops.append(remote(ref, ref, sends(q), recvs(q), at(dp, seg, other)))
        return ops

    def gather_in(block, sends, recvs):
        ops = [remote(block(other), block(other), sends(0), recvs(0), at(dp, seg, other))]
        for q in range(1, pairs):
            i = pairs - 1 + q
            ref = block(came_from(q, 1 - core))
            ops.append(remote(ref, ref, sends(i), recvs(i), at(dp, seg, other)))
        return ops

    def of_sample(m):
        return (
            lambda c: x_block(dp, m, c),
            lambda i: xg_s.at[m, i],
            lambda i: xg_r.at[m, i],
        )

    def of_dp(jd):
        return (
            lambda c: x_block(dp_from(jd), 0, c, mb),
            lambda i: xf_s.at[jd - 1, i],
            lambda i: xf_r.at[jd - 1, i],
        )

    def relay(group):
        for op in relay_in(*group):
            op.wait_recv()
        for op in gather_relay(*group):
            op.start()

    def x_dp(m, j):
        ref = x_block(dp, m, ch)
        return remote(ref, ref, xd_s.at[m, j - 1], xd_r.at[m, j - 1], at(dp_peer(j), seg, ch))

    def x_dp_in(m, j):
        ref = x_block(dp_from(j), m, ch)
        return remote(ref, ref, xd_s.at[m, j - 1], xd_r.at[m, j - 1], at(dp_peer(j), seg, ch))

    def style_dp(j, source):
        ref = styall.at[source]
        return remote(ref, ref, st_s.at[j - 1], st_r.at[j - 1], at(dp_peer(j), seg, ch))

    def coef_dp(j, source):
        ref = coefall.at[source]
        return remote(ref, ref, cf_s.at[j - 1], cf_r.at[j - 1], at(dp_peer(j), seg, ch))

    def image_copy(m, j, source):
        g = lax.rem(me_group + j, ng)
        ref = img.at[m, source]
        return remote(
            ref, ref, im_s.at[m, j - 1], im_r.at[m, j - 1], at(dp, g // nc, lax.rem(g, nc))
        )

    def y_copy(m):
        return remote(ytx.at[m], yin.at[m], yy_s.at[m], yy_r.at[m], at(dp, 1 - seg, ch))

    def ret_copy(m):
        return remote(rettx.at[m], retbuf.at[m], rt_s.at[m], rt_r.at[m], at(dp, 1 - seg, ch))

    def dx_copy(m, j):
        return remote(
            tx.at[m, j - 1],
            rx.at[m, j - 1],
            rs_s.at[m, j - 1],
            rs_r.at[m, j - 1],
            at(dp, seg, chan_peer(j)),
        )

    def gz_block(d, m):
        return gzall.at[:, pl.ds(pl.multiple_of((d * mb + m) * px, px), px)]

    def gz_copy(m, j, source):
        ref = gz_block(source, m)
        return remote(ref, ref, gz_s.at[m, j - 1], gz_r.at[m, j - 1], at(dp_peer(j), seg, ch))

    def send_x(m, value):
        style_col = cols[:, 5 + m : 6 + m]
        own_x(dp, m)[...] = (value.astype(f32) * style_col).astype(bf16)
        for op in gather_out(*of_sample(m)):
            op.start()

    styall[dp] = jnp.zeros((styall.shape[1], full), f32)
    styall[dp, 0:mb, :] = style_ref[0]
    pl.semaphore_wait(barrier, ng - 1 + nd - 1)

    @pl.when(seg == 0)
    def _():
        for m in range(mb):
            send_x(m, base_ref[m])
        for m in range(mb):
            for j in range(1, nd):
                x_dp(m, j).start()

    for j in range(1, nd):
        style_dp(j, dp).start()

    squares = jnp.zeros((ow, full), f32)
    for k in range(9):
        if k == 5:

            @pl.when(seg == 0)
            def _():
                for m in range(mb):
                    relay(of_sample(m))

        block = w_ref[0, k * full : (k + 1) * full, :]
        wcat[:, k * ow : (k + 1) * ow] = block
        turned = block.T
        wt[k * ow : (k + 1) * ow, :] = turned
        wide = turned.astype(f32)
        squares = squares + wide * wide
    for m in range(mb):
        row = style_ref[0, m : m + 1, :]
        total = jnp.sum(squares * (row * row), axis=1, keepdims=True)
        demods[:, m : m + 1] = lax.rsqrt(total + epsilon)
    dpack[...] = jnp.zeros_like(dpack)
    dpack[0:3, :] = dw_ref[...]
    dpack[3:4, :] = db_ref[...]
    dpack[4:5, :] = do_ref[...]
    dcols[...] = dpack[...].T

    @pl.when(seg == 1)
    def _():
        retbuf[...] = jnp.zeros_like(retbuf)
        for m in range(mb):
            y_copy(m).wait_recv()
            send_x(m, yin[m])
        for m in range(mb):
            relay(of_sample(m))
        for m in range(mb):
            for j in range(1, nd):
                x_dp(m, j).start()

    lane = lax.broadcasted_iota(jnp.int32, (1, px), 1)
    pos_y = lane // res
    pos_x = lane % res

    def inside(oy, ox):
        ok_y = (pos_y + oy >= 0) & (pos_y + oy < res)
        ok_x = (pos_x + ox >= 0) & (pos_x + ox < res)
        return ok_y & ok_x

    def shift(value, oy, ox):
        steps = (-(oy * res + ox)) % px
        if steps == 0:
            return value
        return jnp.where(inside(oy, ox), pltpu.roll(value, steps, 1), 0.0)

    for m in range(mb):
        for op in gather_in(*of_sample(m)):
            op.wait_recv()
        x_all = xfull[:, pl.ds(pl.multiple_of((dp * mb + m) * px, px), px)]
        conv = jnp.zeros((ow, px), f32)
        for k, (oy, ox) in enumerate(OFFSETS):
            part = jnp.dot(wt[k * ow : (k + 1) * ow, :], x_all, preferred_element_type=f32)
            conv = conv + shift(part, oy, ox)
        pre = (
            demods[:, m : m + 1] * conv
            + cols[:, 4:5] * noise_ref[0, m : m + 1, :]
            + cols[:, 3:4]
        )
        act, slope = leaky_pair(pre)
        y = (root_two * act).astype(bf16)
        conv_s[m] = conv
        pre_s[m] = root_two * slope

        ytx[m] = y

        @pl.when(seg == 0)
        def _():
            y_copy(m).start()

        img[m, me_group] = jnp.dot(pack[...].astype(bf16), y, preferred_element_type=f32)[0:8]
        for j in range(1, ng):
            image_copy(m, j, me_group).start()

    for m in range(mb):
        for j in range(1, ng):
            image_copy(m, j, lax.rem(me_group + ng - j, ng)).wait_recv()
        total = img[m, 0]
        for g in range(1, ng):
            total = total + img[m, g]
        q = dcols[:, 3:4]
        for c in range(3):
            q = q + dcols[:, c : c + 1] * total[c : c + 1, :]
        act, slope = leaky_pair(q)
        out_col = dcols[:, 4:5]
        logit = jnp.sum(jnp.sum(act, axis=1, keepdims=True) * out_col, axis=0, keepdims=True) / px
        logit_out[m] = jnp.sum(logit)
        e = jnp.exp(-jnp.abs(logit))
        grad = jnp.where(logit >= 0.0, 1.0, e) / (1.0 + e) - 1.0
        dq = (grad * out_col / px) * slope
        for c in range(3):
            dimg[m, c : c + 1, :] = jnp.sum(dcols[:, c : c + 1] * dq, axis=0, keepdims=True)

    def forward_x():
        for jd in range(1, nd):
            for m in range(mb):
                x_dp_in(m, jd).wait_recv()
            for op in gather_out(*of_dp(jd)):
                op.start()

    @pl.when(seg == 0)
    def _():
        forward_x()

    coefall[dp] = jnp.zeros((coefall.shape[1], ow), f32)
    for m in range(mb):

        @pl.when(seg == 0)
        def _():
            ret_copy(m).wait_recv()

        dy = retbuf[m].astype(f32)
        for c in range(3):
            dy = dy + cols[:, c : c + 1] * dimg[m, c : c + 1, :]
        da = dy * pre_s[m]
        demod = demods[:, m : m + 1]
        gz = (da * demod).astype(bf16)
        gz_block(dp, m)[...] = gz
        for j in range(1, nd):
            gz_copy(m, j, dp).start()
        coef = -jnp.sum(da * conv_s[m], axis=1, keepdims=True) * demod * demod * demod
        wide = gz.astype(f32)
        for k, (oy, ox) in enumerate(OFFSETS):
            gst[m, k * ow : (k + 1) * ow, :] = shift(wide, -oy, -ox).astype(bf16)
        for j in range(1, nc):
            rows = pl.ds(pl.multiple_of(chan_peer(j) * ow, ow), ow)
            tx[m, j - 1] = jnp.dot(
                wcat[rows, :], gst[m], preferred_element_type=f32
            ).astype(bf16)
            dx_copy(m, j).start()
        rows = pl.ds(pl.multiple_of(ch * ow, ow), ow)
        dxown[m] = jnp.dot(wcat[rows, :], gst[m], preferred_element_type=f32)
        coefall[dp, m : m + 1, :] = jnp.broadcast_to(coef, (ow, ow)).T[0:1, :]

    for j in range(1, nd):
        coef_dp(j, dp).start()

    for m in range(mb):
        total = dxown[m]
        for j in range(1, nc):
            dx_copy(m, j).wait_recv()
            total = total + rx[m, j - 1].astype(f32)
        returned = (total * cols[:, 5 + m : 6 + m]).astype(bf16)
        ret_out[0, m] = returned
        rettx[m] = returned

        @pl.when(seg == 1)
        def _():
            ret_copy(m).start()

    @pl.when(seg == 1)
    def _():
        forward_x()

    for jd in range(1, nd):
        relay(of_dp(jd))

    rows_out = grad_out.shape[1]
    piece = math.gcd(rows_out, full)
    first_tap = (dp * rows_out) // full
    taps = gt.shape[0]
    for j in range(1, nd):
        for m in range(mb):
            gz_copy(m, j, dp_from(j)).wait_recv()
        style_dp(j, dp_from(j)).wait_recv()
        coef_dp(j, dp_from(j)).wait_recv()
    src = lax.broadcasted_iota(jnp.int32, (px, px), 0)
    dst = lax.broadcasted_iota(jnp.int32, (px, px), 1)
    dst_y, dst_x = dst // res, dst % res
    for t in range(taps):
        k = jnp.minimum(first_tap + t, 8)
        oy, ox = k // 3 - 1, lax.rem(k, 3) - 1
        ok_y = (dst_y - oy >= 0) & (dst_y - oy < res)
        ok_x = (dst_x - ox >= 0) & (dst_x - ox < res)
        hit = (src == dst - (oy * res + ox)) & ok_y & ok_x
        select = jnp.where(hit, 1.0, 0.0).astype(bf16)
        for b in range(nb):
            span = slice(b * px, (b + 1) * px)
            gt[t, :, span] = jnp.dot(
                gzall[:, span], select, preferred_element_type=f32
            ).astype(bf16)
    style_rows = jnp.concatenate([styall[d, 0:mb, :] for d in range(nd)], axis=0)
    style_cols = (style_rows * style_rows).T
    total = jnp.zeros((full, ow), f32)
    for b in range(nb):
        total = total + style_cols[:, b : b + 1] * coefall[b // mb, b % mb : b % mb + 1, :]
    dmat[...] = total
    for jd in range(1, nd):
        for op in gather_in(*of_dp(jd)):
            op.wait_recv()
    for r in range(rows_out // piece):
        start = dp * rows_out + r * piece
        t = start // full - first_tap
        inner = pl.ds(pl.multiple_of(lax.rem(start, full), piece), piece)
        prod = lax.dot_general(
            xfull[inner, :], gt[t], (((1,), (1,)), ((), ())), preferred_element_type=f32
        )
        weight = w_ref[0, pl.ds(pl.multiple_of(start, piece), piece), :].astype(f32)
        grad_out[0, r * piece : (r + 1) * piece, :] = prod + weight * dmat[inner, :]

    for m in range(mb):
        for op in gather_out(*of_sample(m)) + gather_relay(*of_sample(m)):
            op.wait_send()
        for j in range(1, nc):
            dx_copy(m, j).wait_send()
        for j in range(1, ng):
            image_copy(m, j, me_group).wait_send()
        for j in range(1, nd):
            x_dp(m, j).wait_send()
            gz_copy(m, j, dp).wait_send()
    for j in range(1, nd):
        style_dp(j, dp).wait_send()
        coef_dp(j, dp).wait_send()
        for op in gather_out(*of_dp(j)) + gather_relay(*of_dp(j)):
            op.wait_send()

    @pl.when(seg == 0)
    def _():
        for m in range(mb):
            y_copy(m).wait_send()

    @pl.when(seg == 1)
    def _():
        for m in range(mb):
            ret_copy(m).wait_send()


def shards(nd, nc, *args):
    base, style, noise, w, bias, gain, rgb, dw, db, do = args
    mb, ow, px = base.shape
    full = w.shape[1] // 9
    cd = dw.shape[1]
    nb = nd * mb
    rows_out = w.shape[1] // nd
    piece = math.gcd(rows_out, full)
    taps = max(
        ((d + 1) * rows_out - piece) // full - (d * rows_out) // full + 1 for d in range(nd)
    )
    mp = -(-mb // 8) * 8
    dma = pltpu.SemaphoreType.DMA
    pd, pc, pg = max(nd - 1, 1), max(nc - 1, 1), 2 * nc - 1
    vm = pltpu.VMEM
    prow = -(-(5 + mb) // 16) * 16
    scratch = [
        vm((prow, ow), f32),
        vm((ow, prow), f32),
        vm((8, cd), f32),
        vm((cd, 8), f32),
        vm((9 * ow, full), bf16),
        vm((full, 9 * ow), bf16),
        vm((ow, mp), f32),
        vm((mb, ow, px), bf16),
        vm((mb, ow, px), bf16),
        vm((full, nb * px), bf16),
        vm((nd, mp, full), f32),
        vm((nd, mp, ow), f32),
        vm((mb, ow, px), f32),
        vm((mb, ow, px), f32),
        vm((mb, 2 * nc, 8, px), f32),
        vm((mb, 8, px), f32),
        vm((ow, nb * px), bf16),
        vm((mb, 9 * ow, px), bf16),
        vm((mb, pc, ow, px), bf16),
        vm((mb, pc, ow, px), bf16),
        vm((mb, ow, px), f32),
        vm((mb, ow, px), bf16),
        vm((mb, ow, px), bf16),
        vm((taps, ow, nb * px), bf16),
        vm((full, ow), f32),
    ]
    for dims in ((mb, pc), (mb, pd), (pd, pc), (mb, pg), (mb,), (mb, pc), (mb,), (mb, pd), (pd,), (pd,)):
        scratch += [dma(dims), dma(dims)]
    spec = pl.BlockSpec(memory_space=pltpu.VMEM)
    return pl.pallas_call(
        functools.partial(kernel, nd, nc),
        out_shape=(
            jax.ShapeDtypeStruct((1, rows_out, ow), f32),
            jax.ShapeDtypeStruct((mb,), f32),
            jax.ShapeDtypeStruct((1, mb, ow, px), bf16),
        ),
        in_specs=[spec] * 10,
        out_specs=(spec, pl.BlockSpec(memory_space=pltpu.SMEM), spec),
        scratch_shapes=scratch,
        compiler_params=pltpu.CompilerParams(
            collective_id=0, has_side_effects=True, vmem_limit_bytes=56 * 1024 * 1024
        ),
    )(base, style, noise, w, bias, gain, rgb, dw, db[None, :], do[None, :])


def solution(mesh):
    placed = (
        P("dp", "chan", None),
        P("segment", "dp", None),
        P("segment", "dp", None),
        P("segment", None, "chan"),
        P("segment", "chan"),
        P("segment", "chan"),
        P("segment", None, "chan"),
        P(),
        P(),
        P(),
    )
    return jax.shard_map(
        functools.partial(shards, mesh.shape["dp"], mesh.shape["chan"]),
        mesh=mesh,
        in_specs=placed,
        out_specs=(P("segment", "dp", "chan"), P("dp"), P("segment", "dp", "chan", None)),
        check_vma=False,
    )
```

```python
import functools
import math
import jax
import jax.numpy as jnp
from jax import lax
from jax.experimental import pallas as pl
from jax.experimental.pallas import tpu as pltpu
from jax.sharding import PartitionSpec as P

epsilon = 1e-06
root_two = 1.4142135623730951
f32 = jnp.float32
bf16 = jnp.bfloat16
MESH = pl.DeviceIdType.MESH
OFFSETS = [(ky - 1, kx - 1) for ky in range(3) for kx in range(3)]


def leaky_pair(t):
    e = jnp.exp(-jnp.abs(t))
    act = 0.2 * t + 0.8 * (jnp.maximum(t, 0.0) + jnp.log1p(e))
    slope = 0.2 + 0.8 * (jnp.where(t >= 0.0, 1.0, e) / (1.0 + e))
    return act, slope


def remote(src, dst, send_sem, recv_sem, dev):
    return pltpu.make_async_remote_copy(
        src_ref=src,
        dst_ref=dst,
        send_sem=send_sem,
        recv_sem=recv_sem,
        device_id=dev,
        device_id_type=MESH,
    )


def kernel(
    nd,
    nc,
    base_ref,
    style_ref,
    noise_ref,
    w_ref,
    bias_ref,
    gain_ref,
    rgb_ref,
    dw_ref,
    db_ref,
    do_ref,
    grad_out,
    logit_out,
    ret_out,
    pack,
    cols,
    dpack,
    dcols,
    wt,
    wcat,
    demods,
    yin,
    ytx,
    xfull,
    styall,
    coefall,
    conv_s,
    pre_s,
    img,
    dimg,
    gzall,
    gst,
    tx,
    rx,
    dxown,
    retbuf,
    rettx,
    gt,
    dmat,
    sel,
    xg_s,
    xg_r,
    xd_s,
    xd_r,
    xf_s,
    xf_r,
    im_s,
    im_r,
    yy_s,
    yy_r,
    rs_s,
    rs_r,
    rt_s,
    rt_r,
    gz_s,
    gz_r,
    cf_s,
    cf_r,
    st_s,
    st_r,
):
    dp = lax.axis_index("dp")
    seg = lax.axis_index("segment")
    ch = lax.axis_index("chan")
    mb, ow, px = base_ref.shape
    full = w_ref.shape[1] // 9
    res = math.isqrt(px)
    nb = nd * mb
    ng = 2 * nc

    def at(d, s, c):
        return {"dp": d, "segment": s, "chan": c}

    def chan_peer(j):
        return lax.rem(ch + j, nc)

    def chan_from(j):
        return lax.rem(ch + nc - j, nc)

    def dp_peer(j):
        return lax.rem(dp + j, nd)

    def dp_from(j):
        return lax.rem(dp + nd - j, nd)

    me_group = seg * nc + ch

    barrier = pltpu.get_barrier_semaphore()
    for j in range(1, ng):
        g = lax.rem(me_group + j, ng)
        pl.semaphore_signal(
            barrier, inc=1, device_id=at(dp, g // nc, lax.rem(g, nc)), device_id_type=MESH
        )
    for j in range(1, nd):
        pl.semaphore_signal(barrier, inc=1, device_id=at(dp_peer(j), seg, ch), device_id_type=MESH)

    pack[...] = jnp.zeros_like(pack)
    pack[0:3, :] = rgb_ref[0].astype(f32)
    pack[3:4, :] = bias_ref[...]
    pack[4:5, :] = gain_ref[...]
    pack[5 : 5 + mb, :] = style_ref[0, :, pl.ds(pl.multiple_of(ch * ow, ow), ow)]
    cols[...] = pack[...].T

    def own_x(d, m):
        return xfull.at[
            pl.ds(pl.multiple_of(ch * ow, ow), ow),
            pl.ds(pl.multiple_of((d * mb + m) * px, px), px),
        ]

    def x_block(d, m, c, n=1):
        return xfull.at[
            pl.ds(pl.multiple_of(c * ow, ow), ow),
            pl.ds(pl.multiple_of((d * mb + m) * px, px), n * px),
        ]

    pairs = nc // 2
    pair, core = ch // 2, lax.rem(ch, 2)
    other = pair * 2 + 1 - core

    def same_core(q):
        return lax.rem(pair + q, pairs) * 2 + core

    def came_from(q, c):
        return lax.rem(pair + pairs - q, pairs) * 2 + c

    def gather_out(block, sends, recvs):
        ops = [remote(block(ch), block(ch), sends(q), recvs(q), at(dp, seg, same_core(q)))
               for q in range(1, pairs)]
        return ops + [remote(block(ch), block(ch), sends(0), recvs(0), at(dp, seg, other))]

    def gather_relay(block, sends, recvs):
        ops = []
        for q in range(1, pairs):
            i = pairs - 1 + q
            ref = block(came_from(q, core))
            ops.append(remote(ref, ref, sends(i), recvs(i), at(dp, seg, other)))
        return ops

    def relay_in(block, sends, recvs):
        ops = []
        for q in range(1, pairs):
            ref = block(came_from(q, core))
            ops.append(remote(ref, ref, sends(q), recvs(q), at(dp, seg, other)))
        return ops

    def gather_in(block, sends, recvs):
        ops = [remote(block(other), block(other), sends(0), recvs(0), at(dp, seg, other))]
        for q in range(1, pairs):
            i = pairs - 1 + q
            ref = block(came_from(q, 1 - core))
            ops.append(remote(ref, ref, sends(i), recvs(i), at(dp, seg, other)))
        return ops

    def of_sample(m):
        return (
            lambda c: x_block(dp, m, c),
            lambda i: xg_s.at[m, i],
            lambda i: xg_r.at[m, i],
        )

    def of_dp(jd):
        return (
            lambda c: x_block(dp_from(jd), 0, c, mb),
            lambda i: xf_s.at[jd - 1, i],
            lambda i: xf_r.at[jd - 1, i],
        )

    def relay(group):
        for op in relay_in(*group):
            op.wait_recv()
        for op in gather_relay(*group):
            op.start()

    def x_dp(m, j):
        ref = x_block(dp, m, ch)
        return remote(ref, ref, xd_s.at[m, j - 1], xd_r.at[m, j - 1], at(dp_peer(j), seg, ch))

    def x_dp_in(m, j):
        ref = x_block(dp_from(j), m, ch)
        return remote(ref, ref, xd_s.at[m, j - 1], xd_r.at[m, j - 1], at(dp_peer(j), seg, ch))

    def style_dp(j, source):
        ref = styall.at[source]
        return remote(ref, ref, st_s.at[j - 1], st_r.at[j - 1], at(dp_peer(j), seg, ch))

    def coef_dp(j, source):
        ref = coefall.at[source]
        return remote(ref, ref, cf_s.at[j - 1], cf_r.at[j - 1], at(dp_peer(j), seg, ch))

    def image_copy(m, j, source):
        g = lax.rem(me_group + j, ng)
        ref = img.at[m, source]
        return remote(
            ref, ref, im_s.at[m, j - 1], im_r.at[m, j - 1], at(dp, g // nc, lax.rem(g, nc))
        )

    def y_copy(m):
        return remote(ytx.at[m], yin.at[m], yy_s.at[m], yy_r.at[m], at(dp, 1 - seg, ch))

    def ret_copy(m):
        return remote(rettx.at[m], retbuf.at[m], rt_s.at[m], rt_r.at[m], at(dp, 1 - seg, ch))

    def dx_copy(m, i):
        dev = other if i < pairs else same_core(i - pairs + 1)
        return remote(
            tx.at[m, i], rx.at[m, i], rs_s.at[m, i], rs_r.at[m, i], at(dp, seg, dev)
        )

    def gz_block(d, m):
        return gzall.at[:, pl.ds(pl.multiple_of((d * mb + m) * px, px), px)]

    def gz_copy(m, j, source):
        ref = gz_block(source, m)
        return remote(ref, ref, gz_s.at[m, j - 1], gz_r.at[m, j - 1], at(dp_peer(j), seg, ch))

    def send_x(m, value):
        style_col = cols[:, 5 + m : 6 + m]
        own_x(dp, m)[...] = (value.astype(f32) * style_col).astype(bf16)
        for op in gather_out(*of_sample(m)):
            op.start()

    styall[dp] = jnp.zeros((styall.shape[1], full), f32)
    styall[dp, 0:mb, :] = style_ref[0]
    pl.semaphore_wait(barrier, ng - 1 + nd - 1)

    @pl.when(seg == 0)
    def _():
        for m in range(mb):
            send_x(m, base_ref[m])
        for m in range(mb):
            for j in range(1, nd):
                x_dp(m, j).start()

    for j in range(1, nd):
        style_dp(j, dp).start()

    squares = jnp.zeros((ow, full), f32)
    for k in range(9):
        if k == 5:

            @pl.when(seg == 0)
            def _():
                for m in range(mb):
                    relay(of_sample(m))

        block = w_ref[0, k * full : (k + 1) * full, :]
        wcat[:, k * ow : (k + 1) * ow] = block
        turned = block.T
        wt[k * ow : (k + 1) * ow, :] = turned
        wide = turned.astype(f32)
        squares = squares + wide * wide
    for m in range(mb):
        row = style_ref[0, m : m + 1, :]
        total = jnp.sum(squares * (row * row), axis=1, keepdims=True)
        demods[:, m : m + 1] = lax.rsqrt(total + epsilon)
    dpack[...] = jnp.zeros_like(dpack)
    dpack[0:3, :] = dw_ref[...]
    dpack[3:4, :] = db_ref[...]
    dpack[4:5, :] = do_ref[...]
    dcols[...] = dpack[...].T

    @pl.when(seg == 1)
    def _():
        retbuf[...] = jnp.zeros_like(retbuf)
        for m in range(mb):
            y_copy(m).wait_recv()
            send_x(m, yin[m])
        for m in range(mb):
            relay(of_sample(m))
        for m in range(mb):
            for j in range(1, nd):
                x_dp(m, j).start()

    lane = lax.broadcasted_iota(jnp.int32, (1, px), 1)
    pos_y = lane // res
    pos_x = lane % res

    def inside(oy, ox):
        ok_y = (pos_y + oy >= 0) & (pos_y + oy < res)
        ok_x = (pos_x + ox >= 0) & (pos_x + ox < res)
        return ok_y & ok_x

    def shift(value, oy, ox):
        steps = (-(oy * res + ox)) % px
        if steps == 0:
            return value
        return jnp.where(inside(oy, ox), pltpu.roll(value, steps, 1), 0.0)

    for m in range(mb):
        for op in gather_in(*of_sample(m)):
            op.wait_recv()
        x_all = xfull[:, pl.ds(pl.multiple_of((dp * mb + m) * px, px), px)]
        conv = jnp.zeros((ow, px), f32)
        for k, (oy, ox) in enumerate(OFFSETS):
            part = jnp.dot(wt[k * ow : (k + 1) * ow, :], x_all, preferred_element_type=f32)
            conv = conv + shift(part, oy, ox)
        pre = (
            demods[:, m : m + 1] * conv
            + cols[:, 4:5] * noise_ref[0, m : m + 1, :]
            + cols[:, 3:4]
        )
        act, slope = leaky_pair(pre)
        y = (root_two * act).astype(bf16)
        conv_s[m] = conv
        pre_s[m] = root_two * slope

        ytx[m] = y

        @pl.when(seg == 0)
        def _():
            y_copy(m).start()

        img[m, me_group] = jnp.dot(pack[...].astype(bf16), y, preferred_element_type=f32)[0:8]
        for j in range(1, ng):
            image_copy(m, j, me_group).start()

    for m in range(mb):
        for j in range(1, ng):
            image_copy(m, j, lax.rem(me_group + ng - j, ng)).wait_recv()
        total = img[m, 0]
        for g in range(1, ng):
            total = total + img[m, g]
        q = dcols[:, 3:4]
        for c in range(3):
            q = q + dcols[:, c : c + 1] * total[c : c + 1, :]
        act, slope = leaky_pair(q)
        out_col = dcols[:, 4:5]
        logit = jnp.sum(jnp.sum(act, axis=1, keepdims=True) * out_col, axis=0, keepdims=True) / px
        logit_out[m] = jnp.sum(logit)
        e = jnp.exp(-jnp.abs(logit))
        grad = jnp.where(logit >= 0.0, 1.0, e) / (1.0 + e) - 1.0
        dq = (grad * out_col / px) * slope
        for c in range(3):
            dimg[m, c : c + 1, :] = jnp.sum(dcols[:, c : c + 1] * dq, axis=0, keepdims=True)

    rows_out = grad_out.shape[1]
    first_tap = (dp * rows_out) // full
    taps = gt.shape[0]

    def make_selects():
        src = lax.broadcasted_iota(jnp.int32, (px, px), 0)
        dst = lax.broadcasted_iota(jnp.int32, (px, px), 1)
        dst_y, dst_x = dst // res, dst % res
        for t in range(taps):
            k = jnp.minimum(first_tap + t, 8)
            oy, ox = k // 3 - 1, lax.rem(k, 3) - 1
            ok_y = (dst_y - oy >= 0) & (dst_y - oy < res)
            ok_x = (dst_x - ox >= 0) & (dst_x - ox < res)
            hit = (src == dst - (oy * res + ox)) & ok_y & ok_x
            sel[t] = jnp.where(hit, 1.0, 0.0).astype(bf16)

    def forward_x():
        for jd in range(1, nd):
            for m in range(mb):
                x_dp_in(m, jd).wait_recv()
            for op in gather_out(*of_dp(jd)):
                op.start()

    @pl.when(seg == 0)
    def _():
        forward_x()
        make_selects()

    coefall[dp] = jnp.zeros((coefall.shape[1], ow), f32)
    for m in range(mb):

        @pl.when(seg == 0)
        def _():
            ret_copy(m).wait_recv()

        dy = retbuf[m].astype(f32)
        for c in range(3):
            dy = dy + cols[:, c : c + 1] * dimg[m, c : c + 1, :]
        da = dy * pre_s[m]
        demod = demods[:, m : m + 1]
        gz = (da * demod).astype(bf16)
        gz_block(dp, m)[...] = gz
        for j in range(1, nd):
            gz_copy(m, j, dp).start()
        coef = -jnp.sum(da * conv_s[m], axis=1, keepdims=True) * demod * demod * demod
        wide = gz.astype(f32)
        for k, (oy, ox) in enumerate(OFFSETS):
            gst[m, k * ow : (k + 1) * ow, :] = shift(wide, -oy, -ox).astype(bf16)

        def part(c):
            rows = pl.ds(pl.multiple_of(c * ow, ow), ow)
            return jnp.dot(wcat[rows, :], gst[m], preferred_element_type=f32)

        for q in range(1, pairs):
            tx[m, q] = part(lax.rem(pair + q, pairs) * 2 + 1 - core).astype(bf16)
            dx_copy(m, q).start()
        mine = [part(same_core(q)) for q in range(1, pairs)]
        tx[m, 0] = part(other).astype(bf16)
        dx_copy(m, 0).start()
        dxown[m] = part(ch)
        for q in range(1, pairs):
            i = pairs - 1 + q
            dx_copy(m, q).wait_recv()
            tx[m, i] = (mine[q - 1] + rx[m, q].astype(f32)).astype(bf16)
            dx_copy(m, i).start()
        coefall[dp, m : m + 1, :] = jnp.broadcast_to(coef, (ow, ow)).T[0:1, :]

    for j in range(1, nd):
        coef_dp(j, dp).start()

    for m in range(mb):
        total = dxown[m]
        for i in [0] + list(range(pairs, nc - 1)):
            dx_copy(m, i).wait_recv()
            total = total + rx[m, i].astype(f32)
        returned = (total * cols[:, 5 + m : 6 + m]).astype(bf16)
        ret_out[0, m] = returned
        rettx[m] = returned

        @pl.when(seg == 1)
        def _():
            ret_copy(m).start()

    @pl.when(seg == 1)
    def _():
        forward_x()
        make_selects()

    for jd in range(1, nd):
        relay(of_dp(jd))

    piece = math.gcd(rows_out, full)
    for m in range(mb):
        for j in range(nd):
            if j > 0:
                gz_copy(m, j, dp_from(j)).wait_recv()
            span = pl.ds(pl.multiple_of((dp_from(j) * mb + m) * px, px), px)
            for t in range(taps):
                gt[t, :, span] = jnp.dot(
                    gzall[:, span], sel[t], preferred_element_type=f32
                ).astype(bf16)
    for j in range(1, nd):
        style_dp(j, dp_from(j)).wait_recv()
        coef_dp(j, dp_from(j)).wait_recv()
    style_rows = jnp.concatenate([styall[d, 0:mb, :] for d in range(nd)], axis=0)
    style_cols = (style_rows * style_rows).T
    total = jnp.zeros((full, ow), f32)
    for b in range(nb):
        total = total + style_cols[:, b : b + 1] * coefall[b // mb, b % mb : b % mb + 1, :]
    dmat[...] = total
    for jd in range(1, nd):
        for op in gather_in(*of_dp(jd)):
            op.wait_recv()
    for r in range(rows_out // piece):
        start = dp * rows_out + r * piece
        t = start // full - first_tap
        inner = pl.ds(pl.multiple_of(lax.rem(start, full), piece), piece)
        prod = lax.dot_general(
            xfull[inner, :], gt[t], (((1,), (1,)), ((), ())), preferred_element_type=f32
        )
        weight = w_ref[0, pl.ds(pl.multiple_of(start, piece), piece), :].astype(f32)
        grad_out[0, r * piece : (r + 1) * piece, :] = prod + weight * dmat[inner, :]

    for m in range(mb):
        for op in gather_out(*of_sample(m)) + gather_relay(*of_sample(m)):
            op.wait_send()
        for i in range(nc - 1):
            dx_copy(m, i).wait_send()
        for j in range(1, ng):
            image_copy(m, j, me_group).wait_send()
        for j in range(1, nd):
            x_dp(m, j).wait_send()
            gz_copy(m, j, dp).wait_send()
    for j in range(1, nd):
        style_dp(j, dp).wait_send()
        coef_dp(j, dp).wait_send()
        for op in gather_out(*of_dp(j)) + gather_relay(*of_dp(j)):
            op.wait_send()

    @pl.when(seg == 0)
    def _():
        for m in range(mb):
            y_copy(m).wait_send()

    @pl.when(seg == 1)
    def _():
        for m in range(mb):
            ret_copy(m).wait_send()


def shards(nd, nc, *args):
    base, style, noise, w, bias, gain, rgb, dw, db, do = args
    mb, ow, px = base.shape
    full = w.shape[1] // 9
    cd = dw.shape[1]
    nb = nd * mb
    rows_out = w.shape[1] // nd
    piece = math.gcd(rows_out, full)
    taps = max(
        ((d + 1) * rows_out - piece) // full - (d * rows_out) // full + 1 for d in range(nd)
    )
    mp = -(-mb // 8) * 8
    dma = pltpu.SemaphoreType.DMA
    pd, pc, pg = max(nd - 1, 1), max(nc - 1, 1), 2 * nc - 1
    vm = pltpu.VMEM
    prow = -(-(5 + mb) // 16) * 16
    scratch = [
        vm((prow, ow), f32),
        vm((ow, prow), f32),
        vm((8, cd), f32),
        vm((cd, 8), f32),
        vm((9 * ow, full), bf16),
        vm((full, 9 * ow), bf16),
        vm((ow, mp), f32),
        vm((mb, ow, px), bf16),
        vm((mb, ow, px), bf16),
        vm((full, nb * px), bf16),
        vm((nd, mp, full), f32),
        vm((nd, mp, ow), f32),
        vm((mb, ow, px), f32),
        vm((mb, ow, px), f32),
        vm((mb, 2 * nc, 8, px), f32),
        vm((mb, 8, px), f32),
        vm((ow, nb * px), bf16),
        vm((mb, 9 * ow, px), bf16),
        vm((mb, pc, ow, px), bf16),
        vm((mb, pc, ow, px), bf16),
        vm((mb, ow, px), f32),
        vm((mb, ow, px), bf16),
        vm((mb, ow, px), bf16),
        vm((taps, ow, nb * px), bf16),
        vm((full, ow), f32),
        vm((taps, px, px), bf16),
    ]
    for dims in ((mb, pc), (mb, pd), (pd, pc), (mb, pg), (mb,), (mb, pc), (mb,), (mb, pd), (pd,), (pd,)):
        scratch += [dma(dims), dma(dims)]
    spec = pl.BlockSpec(memory_space=pltpu.VMEM)
    return pl.pallas_call(
        functools.partial(kernel, nd, nc),
        out_shape=(
            jax.ShapeDtypeStruct((1, rows_out, ow), f32),
            jax.ShapeDtypeStruct((mb,), f32),
            jax.ShapeDtypeStruct((1, mb, ow, px), bf16),
        ),
        in_specs=[spec] * 10,
        out_specs=(spec, pl.BlockSpec(memory_space=pltpu.SMEM), spec),
        scratch_shapes=scratch,
        compiler_params=pltpu.CompilerParams(
            collective_id=0, has_side_effects=True, vmem_limit_bytes=56 * 1024 * 1024
        ),
    )(base, style, noise, w, bias, gain, rgb, dw, db[None, :], do[None, :])


def solution(mesh):
    placed = (
        P("dp", "chan", None),
        P("segment", "dp", None),
        P("segment", "dp", None),
        P("segment", None, "chan"),
        P("segment", "chan"),
        P("segment", "chan"),
        P("segment", None, "chan"),
        P(),
        P(),
        P(),
    )
    return jax.shard_map(
        functools.partial(shards, mesh.shape["dp"], mesh.shape["chan"]),
        mesh=mesh,
        in_specs=placed,
        out_specs=(P("segment", "dp", "chan"), P("dp"), P("segment", "dp", "chan", None)),
        check_vma=False,
    )
```
